32 devices in a mesh: group: 2 (over x), pos: 16 (over z, y, core).
Axes of the slice: x: 2, y: 2, z: 4, core: 2. Of those that a mesh axis runs over, the one named last changes fastest.
Arguments:
- acts: bfloat16 [4, 1024, 1536], P('group', 'pos'), parts along dimension 0, may hold values from -12 to 12
- skips: bfloat16 [4, 2048, 1280], P('group', 'pos'), parts along dimension 0, may hold values from -6 to 6
- norm_gain: float32 [1536], replicated, may hold values from 0.6 to 1.6
- w_query: bfloat16 [1536, 256], replicated, may hold values from -4 to 4
- w_key: bfloat16 [1536, 256], replicated, may hold values from -4 to 4
- w_value: bfloat16 [1536, 768], replicated, may hold values from -0.15625 to 0.15625
- w_out: bfloat16 [768, 1536], replicated, may hold values from -0.21875 to 0.21875
- w_lift: bfloat16 [1536, 1536], P('pos'), may hold values from -0.15625 to 0.15625
- w_skip: bfloat16 [1280, 1536], P('pos'), may hold values from -0.15625 to 0.15625
- depth_kernel: float32 [3, 1536], replicated, may hold values from -3 to 3
- w_point: bfloat16 [1536, 1536], P(None, 'pos'), may hold values from -0.15625 to 0.15625
Outputs:
- decoded: bfloat16 [4, 2048, 1536], P('group', 'pos'), parts along dimension 0
The draws below stay inside these ranges and needn't reach their ends.
There are 2 independent parts, one for each index of `group`. The reference program is written for one: setup_inputs(seed, part) draws one part's arguments, and reference() takes and returns one part's arrays. A program takes and returns all parts, laid end to end along the dimension named above; an argument that names none is the same for every part. Nothing has to cross between parts.
All inputs are finite; a program needn't handle non-finite values.
Results may differ from the reference program's by a relative error of at most 0.014.
Values may be sent and summed in bfloat16 or wider, within the bound.
A program may use at most 128 MiB of HBM per device.

```python
import jax
import jax.numpy as jnp
from jax import lax

D = 1536
CS = 1280
HEADS = 4
HK = 64
HV = 192
SEQS = 2
BINS = 1024


def marked_layout(feature_count, head_count):
    per_head = 8
    spacing = feature_count // (per_head * head_count)
    slot_ids = jnp.arange(per_head * head_count, dtype=jnp.int32)
    owner_head = slot_ids % head_count
    sign_values = jnp.where(slot_ids // head_count % 2 == 0, 1.0, -1.0).astype(jnp.float32)
    pattern = jnp.zeros((head_count, feature_count), jnp.float32)
    return pattern.at[owner_head, slot_ids * spacing].set(sign_values / jnp.sqrt(jnp.float32(per_head)))


def unit_rows(raw_noise, support):
    free_count = raw_noise.shape[-1] - jnp.sum(support.astype(jnp.float32))
    raw_noise = jnp.where(support, 0.0, raw_noise)
    raw_noise = raw_noise - jnp.sum(raw_noise, axis=-1, keepdims=True) / free_count
    raw_noise = jnp.where(support, 0.0, raw_noise)
    return raw_noise * jnp.sqrt(raw_noise.shape[-1] / jnp.sum(raw_noise * raw_noise, axis=-1, keepdims=True))


def draw_acts(key, part):
    pattern = marked_layout(D, HEADS)
    support = jnp.sum(jnp.abs(pattern), axis=0) > 0.0
    direction = jnp.sum(pattern, axis=0) / jnp.sqrt(jnp.float32(HEADS))
    noise_key, place_key, level_key = jax.random.split(key, 3)
    raw_noise = jnp.clip(jax.random.normal(noise_key, (SEQS, BINS, D), jnp.float32), -4.0, 4.0)
    unit_noise = unit_rows(raw_noise, support)
    starts = jax.random.randint(place_key, (SEQS,), 0, BINS - 5).astype(jnp.int32)
    places = (starts[:, None] + jnp.arange(6, dtype=jnp.int32)[None, :]).astype(jnp.int32)
    tier_levels = 0.955 + 0.01 * jnp.arange(3, dtype=jnp.float32)
    upper_level = tier_levels[None, :] + jax.random.uniform(level_key, (SEQS, 3), jnp.float32, 0.0, 0.006)
    levels = jnp.stack([upper_level, upper_level - 0.0085], axis=-1).reshape(SEQS, 6)
    chosen = jnp.take_along_axis(unit_noise, places[:, :, None], axis=1)
    marked = levels[..., None] * jnp.sqrt(jnp.float32(D)) * direction + jnp.sqrt(1.0 - levels * levels)[..., None] * chosen
    seq_rows = jnp.arange(SEQS, dtype=jnp.int32)[:, None]
    drawn_acts = unit_noise.at[seq_rows, places].set(marked)
    return drawn_acts.astype(jnp.bfloat16)


def draw_norm_gain(key, part):
    pattern = marked_layout(D, HEADS)
    support = jnp.sum(jnp.abs(pattern), axis=0) > 0.0
    wide_key, steady_key = jax.random.split(jax.random.fold_in(key, 3))
    wide_gain = jax.random.uniform(wide_key, (D,), jnp.float32, 0.6, 1.4)
    steady_gain = jax.random.uniform(steady_key, (D,), jnp.float32, 0.97, 1.03)
    return jnp.where(support, steady_gain, wide_gain)


def query_key_weight(key, offset_id):
    pattern = marked_layout(D, HEADS)
    support = jnp.sum(jnp.abs(pattern), axis=0) > 0.0
    angle_key, order_key = jax.random.split(jax.random.fold_in(key, 7))
    heading = jax.random.normal(angle_key, (HEADS, HK), jnp.float32)
    heading = heading / jnp.sqrt(jnp.sum(heading * heading, axis=-1, keepdims=True))
    ranking = jax.random.permutation(order_key, HEADS).astype(jnp.float32)
    strength = 0.5 + 0.5 * ranking / max(HEADS - 1, 1)
    factor = jnp.sqrt(320.0 * HEADS * jnp.sqrt(jnp.float32(HK)) / D)
    column_scale = 1.33 * jnp.exp(jax.random.uniform(jax.random.fold_in(key, 9), (HEADS, HK), jnp.float32, jnp.log(0.5), jnp.log(2.0)))
    random_part = jnp.clip(jax.random.normal(jax.random.fold_in(key, offset_id), (D, HEADS, HK), jnp.float32), -6.0, 6.0) / jnp.sqrt(jnp.float32(D))
    random_part = random_part * column_scale[None]
    random_part = jnp.where(support[:, None, None], 0.0, random_part)
    component = jnp.sum(random_part * heading[None], axis=-1, keepdims=True)
    remaining = random_part - component * heading[None]
    planted = factor * pattern.T[:, :, None] * (jnp.sqrt(strength)[:, None] * heading)[None]
    return (remaining + planted).reshape(D, HEADS * HK)


def draw_w_query(key, part):
    return query_key_weight(key, 21).astype(jnp.bfloat16)


def draw_w_key(key, part):
    return query_key_weight(key, 22).astype(jnp.bfloat16)


def level_of(key, shape, pieces, least, high):
    level, own = 1.0, jax.random.fold_in(key, 6)
    for dim, blocks in pieces:
        draws = jnp.exp(jax.random.uniform(jax.random.fold_in(own, dim), (blocks,), jnp.float32, least / len(pieces), high / len(pieces)))
        level = level * jnp.repeat(draws, shape[dim] // blocks).reshape([-1 if axis == dim else 1 for axis in range(len(shape))])
    return level


def normal_values(rng, dims, scale, reach, pieces=(), held_as=jnp.bfloat16):
    entries = jax.random.normal(rng, dims, jnp.float32) * scale
    if len(pieces) > 0:
        entries = level_of(rng, dims, pieces, -0.22, 0.18) * entries
    return jnp.clip(entries, min=-reach, max=reach).astype(held_as)


def setup_inputs(seed: int = 0, part: int = 0) -> dict:
    keys = jax.random.split(jax.random.key(seed), 12)
    own_keys = jax.random.split(jax.random.fold_in(keys[11], part), 12)
    acts = draw_acts(jax.random.fold_in(jax.random.fold_in(keys[11], part), 71), part)
    skips = normal_values(own_keys[1], (SEQS, 2 * BINS, CS), 1.0, 6.0, ((1, 16),))
    norm_gain = draw_norm_gain(jax.random.fold_in(keys[11], 71), part)
    w_query = draw_w_query(jax.random.fold_in(keys[11], 71), part)
    w_key = draw_w_key(jax.random.fold_in(keys[11], 71), part)
    w_value = normal_values(keys[5], (D, HEADS * HV), D ** -0.5, 0.15625)
    w_out = normal_values(keys[6], (HEADS * HV, D), (HEADS * HV) ** -0.5, 0.21875)
    w_lift = normal_values(keys[7], (D, D), D ** -0.5, 0.15625, ((0, 16),))
    w_skip = normal_values(keys[8], (CS, D), CS ** -0.5, 0.15625, ((0, 16),))
    depth_kernel = normal_values(keys[9], (3, D), 0.6, 3.0, (), jnp.float32)
    w_point = normal_values(keys[10], (D, D), D ** -0.5, 0.15625, ((1, 16),))
    return dict(acts=acts, skips=skips, norm_gain=norm_gain, w_query=w_query, w_key=w_key, w_value=w_value, w_out=w_out, w_lift=w_lift, w_skip=w_skip, depth_kernel=depth_kernel, w_point=w_point)


def reference(acts, skips, norm_gain, w_query, w_key, w_value, w_out, w_lift, w_skip, depth_kernel, w_point):
    actsf = acts.astype(jnp.float32)
    centre = actsf - lax.optimization_barrier(jnp.mean(actsf, axis=-1, keepdims=True))
    normed = (centre * lax.rsqrt(lax.optimization_barrier(jnp.mean(centre * centre, axis=-1, keepdims=True)) + 1e-05) * norm_gain).astype(jnp.bfloat16)
    flat = normed.reshape(SEQS * BINS, D)
    queries = (jnp.dot(flat, w_query, preferred_element_type=jnp.float32) * HK ** (-0.5)).astype(jnp.bfloat16).reshape(SEQS, BINS, HEADS, HK)
    keyed = jnp.dot(flat, w_key, preferred_element_type=jnp.float32).astype(jnp.bfloat16).reshape(SEQS, BINS, HEADS, HK)
    valued = jnp.dot(flat, w_value, preferred_element_type=jnp.float32).astype(jnp.bfloat16).reshape(SEQS, BINS, HEADS, HV)
    block = min(512, BINS)
    nblocks = BINS // block

    def attend(index):
        part = lax.dynamic_slice_in_dim(queries, (index * block).astype(jnp.int32), block, 1)
        scores = jnp.einsum('sqhd,skhd->shqk', part.astype(jnp.float32), keyed.astype(jnp.float32))
        highest = lax.optimization_barrier(jnp.max(scores, axis=-1, keepdims=True))
        weights = jnp.exp(scores - highest)
        totals = lax.optimization_barrier(jnp.sum(weights, axis=-1))
        summed = jnp.einsum('shqk,skhv->shqv', weights.astype(jnp.bfloat16).astype(jnp.float32), valued.astype(jnp.float32))
        return (summed / totals[..., None]).transpose(0, 2, 1, 3)
    blocks = lax.map(attend, jnp.arange(nblocks, dtype=jnp.int32))
    mixed = blocks.transpose(1, 0, 2, 3, 4).reshape(SEQS * BINS, HEADS * HV).astype(jnp.bfloat16)
    attended = (actsf.reshape(SEQS * BINS, D) + jnp.dot(mixed, w_out, preferred_element_type=jnp.float32)).astype(jnp.bfloat16)
    activated = jax.nn.gelu(attended.astype(jnp.float32)).astype(jnp.bfloat16)
    lifted = jnp.dot(activated, w_lift, preferred_element_type=jnp.float32).astype(jnp.bfloat16).reshape(SEQS, BINS, D)
    raised = jnp.repeat(lifted, 2, axis=1).reshape(SEQS * 2 * BINS, D)
    skip_act = jax.nn.gelu(skips.astype(jnp.float32)).astype(jnp.bfloat16).reshape(SEQS * 2 * BINS, CS)
    merged = (raised.astype(jnp.float32) + jnp.dot(skip_act, w_skip, preferred_element_type=jnp.float32)).astype(jnp.bfloat16).reshape(SEQS, 2 * BINS, D)
    padded = jnp.pad(merged.astype(jnp.float32), ((0, 0), (1, 1), (0, 0)))
    spread = (depth_kernel[0] * padded[:, :-2] + depth_kernel[1] * padded[:, 1:-1] + depth_kernel[2] * padded[:, 2:]).astype(jnp.bfloat16)
    decoded = jnp.dot(spread.reshape(SEQS * 2 * BINS, D), w_point, preferred_element_type=jnp.float32)
    return decoded.astype(jnp.bfloat16).reshape(SEQS, 2 * BINS, D)
```

```python
import functools

import jax
import jax.numpy as jnp
from jax import lax
from jax.experimental import pallas as pl
from jax.experimental.pallas import tpu as pltpu
from jax.sharding import PartitionSpec as P

HEADS = 4
HK = 64
HV = 192


def extended(cells, sides, width):
    for axis, dim in sides:
        count = lax.axis_size(axis)
        ends = count - 1
        head = lax.slice_in_dim(cells, 0, width, axis=dim)
        tail = lax.slice_in_dim(cells, cells.shape[dim] - width, cells.shape[dim], axis=dim)
        cells = jnp.concatenate(
            [
                lax.ppermute(tail, axis, [(i, (i + 1) % count) for i in range(ends)]),
                cells,
                lax.ppermute(head, axis, [((i + 1) % count, i) for i in range(ends)]),
            ],
            axis=dim,
        )
    return cells


def on_device(
    acts, skips, norm_gain, w_query, w_key, w_value, w_out, w_lift, w_skip, depth_kernel, w_point
):
    lift_full, skip_full, point_full = (
        lax.all_gather(w_lift, "pos", axis=0, tiled=True),
        lax.all_gather(w_skip, "pos", axis=0, tiled=True),
        lax.all_gather(w_point, "pos", axis=1, tiled=True),
    )
    seq_count, bin_rows, width = acts.shape
    actsf = acts.astype(jnp.float32)
    centre = actsf - jnp.mean(actsf, axis=-1, keepdims=True)
    normed = (
        centre * lax.rsqrt(jnp.mean(centre * centre, axis=-1, keepdims=True) + 1e-05) * norm_gain
    ).astype(jnp.bfloat16)
    flat = normed.reshape(seq_count * bin_rows, width)
    queries = (
        (jnp.dot(flat, w_query, preferred_element_type=jnp.float32) * HK ** (-0.5))
        .astype(jnp.bfloat16)
        .reshape(seq_count, bin_rows, HEADS, HK)
    )
    keys_here = (
        jnp.dot(flat, w_key, preferred_element_type=jnp.float32)
        .astype(jnp.bfloat16)
        .reshape(seq_count, bin_rows, HEADS * HK)
    )
    values_here = (
        jnp.dot(flat, w_value, preferred_element_type=jnp.float32)
        .astype(jnp.bfloat16)
        .reshape(seq_count, bin_rows, HEADS * HV)
    )
    running = jnp.full((seq_count, HEADS, bin_rows), -1e30, jnp.float32)
    key_piece = lax.all_gather(keys_here, "pos", axis=1, tiled=True)
    value_piece = lax.all_gather(values_here, "pos", axis=1, tiled=True)
    count = key_piece.shape[1]
    keyed = key_piece.reshape(seq_count, count, HEADS, HK)
    valued = value_piece.reshape(seq_count, count, HEADS, HV)
    scores = jnp.einsum("sqhd,skhd->shqk", queries, keyed, preferred_element_type=jnp.float32)
    newest = jnp.maximum(running, jnp.max(scores, axis=-1))
    weights = jnp.exp(scores - newest[..., None])
    totals = jnp.sum(weights, axis=-1)
    summed = jnp.einsum(
        "shqk,skhv->shqv", weights.astype(jnp.bfloat16), valued, preferred_element_type=jnp.float32
    )
    running, totals, summed = (newest, totals, summed)
    mixed = (
        (summed / totals[..., None])
        .transpose(0, 2, 1, 3)
        .reshape(seq_count * bin_rows, HEADS * HV)
        .astype(jnp.bfloat16)
    )
    attended = (
        actsf.reshape(seq_count * bin_rows, width)
        + jnp.dot(mixed, w_out, preferred_element_type=jnp.float32)
    ).astype(jnp.bfloat16)
    activated = jax.nn.gelu(attended.astype(jnp.float32)).astype(jnp.bfloat16)
    lifted = jnp.dot(activated, lift_full, preferred_element_type=jnp.float32)
    lifted = lifted.astype(jnp.bfloat16).reshape(seq_count, bin_rows, width)
    raised = jnp.repeat(lifted, 2, axis=1).reshape(seq_count * 2 * bin_rows, width)
    skip_act = (
        jax.nn.gelu(skips.astype(jnp.float32))
        .astype(jnp.bfloat16)
        .reshape(seq_count * 2 * bin_rows, skips.shape[2])
    )
    skip_term = jnp.dot(skip_act, skip_full, preferred_element_type=jnp.float32)
    merged = (
        (raised.astype(jnp.float32) + skip_term)
        .astype(jnp.bfloat16)
        .reshape(seq_count, 2 * bin_rows, width)
    )
    padded = extended(merged, (("pos", 1),), 1)
    paddedf = padded.astype(jnp.float32)
    spread = (
        depth_kernel[0] * paddedf[:, :-2]
        + depth_kernel[1] * paddedf[:, 1:-1]
        + depth_kernel[2] * paddedf[:, 2:]
    ).astype(jnp.bfloat16)
    spread = spread.reshape(seq_count * 2 * bin_rows, width)
    decoded = jnp.dot(spread, point_full, preferred_element_type=jnp.float32)
    return decoded.astype(jnp.bfloat16).reshape(seq_count, 2 * bin_rows, width)


SEND_RING, SEND_SIDE, SEND_CROSS = 0, 1, 2
KV, SKIP, MINE, THEIRS = 0, 1, 2, 3
MESH = pl.DeviceIdType.MESH


def fused_kernel(
    groups, places,
    acts_h, skips_h, gain_ref, wq_h, wk_h, wv_h, wo_h, lift_h, point_h, skip_h, depth_ref,
    out_ref,
    acts, skips, wq, wk, wv, wo, pair, skip_full, kv, normed, queries, mixed, activated,
    skip_act, term, spread, halo_out, halo_in,
    local_sem, send_sem, recv_sem, halo_send, halo_recv,
):
    chips = places // 2
    reach = chips // 2
    me, group = lax.axis_index("pos"), lax.axis_index("group")
    core, chip = lax.rem(me, 2), lax.div(me, 2)
    column, level = lax.rem(chip, 2), lax.div(chip, 2)
    ring = level + column * (chips - 1 - 2 * level)
    mine = lax.rem(group, 2)
    partner = group + 1 - 2 * mine
    side = chip * 2 + 1 - core
    width = acts.shape[1]
    skip_rows, pair_rows, bins = skip_h.shape[0], lift_h.shape[0], acts.shape[0] // 2

    def chip_at(place):
        place = lax.rem(place + chips, chips)
        far = lax.div(place, reach)
        return (1 - far) * 2 * place + far * (2 * (chips - 1 - place) + 1)

    right, left = chip_at(ring + 1) * 2 + core, chip_at(ring - 1) * 2 + core

    def origin(way, hops, of_core):
        return chip_at(ring - hops if way == 0 else ring + hops) * 2 + of_core

    def view(array, device, part):
        if array == KV:
            if part is None:
                return kv.at[device]
            return kv.at[device, pl.ds(part * bins, bins)]
        rows = skip_rows if array == SKIP else pair_rows
        first = (rows // 2 + 15) // 16 * 16
        start, size = ((0, rows), (0, first), (first, rows - first))[0 if part is None else part + 1]
        window = pl.ds(pl.multiple_of(device * rows + start, 16), size)
        if array == SKIP:
            return skip_full.at[window]
        return pair.at[mine if array == MINE else 1 - mine, window]

    def slot(way, hops):
        return way * reach + hops - 1

    def part_of(way, hops):
        return way if hops == reach else None

    own_slot = 2 * reach
    sent = []

    def send(array, ref, kind, index, target, at_array=None):
        at_array = array if at_array is None else at_array
        copy = pltpu.make_async_remote_copy(
            src_ref=ref,
            dst_ref=ref,
            send_sem=send_sem.at[array, kind, index],
            recv_sem=recv_sem.at[at_array, 1 if kind == SEND_SIDE else 0, index],
            device_id=target,
            device_id_type=MESH,
        )
        copy.start()
        sent.append(copy)

    def arrived(array, plane, index, ref):
        pltpu.make_async_remote_copy(
            src_ref=ref,
            dst_ref=ref,
            send_sem=send_sem.at[array, 0, index],
            recv_sem=recv_sem.at[array, plane, index],
            device_id={"pos": side},
            device_id_type=MESH,
        ).wait_recv()

    def onward(array, way, hops):
        if hops < reach:
            ref = view(array, origin(way, hops, core), part_of(way, hops + 1))
            send(array, ref, SEND_RING, slot(way, hops + 1), {"pos": right if way == 0 else left})

    def pump(array, hops):
        for way in (0, 1):
            ref = view(array, origin(way, hops, core), part_of(way, hops))
            arrived(array, 0, slot(way, hops), ref)
            if array != THEIRS:
                onward(array, way, hops)
            if array == MINE:
                send(array, ref, SEND_CROSS, slot(way, hops), {"group": partner}, THEIRS)
            send(array, ref, SEND_SIDE, slot(way, hops), {"pos": side})

    def begin(array):
        if array != THEIRS:
            onward(array, 0, 0)
            onward(array, 1, 0)
        send(array, view(array, me, None), SEND_SIDE, own_slot, {"pos": side})

    def from_side(array):
        arrived(array, 1, own_slot, view(array, side, None))
        for hops in range(1, reach + 1):
            for way in (0, 1):
                ref = view(array, origin(way, hops, 1 - core), part_of(way, hops))
                arrived(array, 1, slot(way, hops), ref)

    def fetch(index, source, target):
        copy = pltpu.make_async_copy(source, target, local_sem.at[index])
        copy.start()
        return copy

    own_pair = pl.ds(pl.multiple_of(me * pair_rows, 16), pair_rows)
    own_skip = pl.ds(pl.multiple_of(me * skip_rows, 16), skip_rows)
    shards = [
        fetch(0, lift_h, pair.at[0, own_pair]),
        fetch(1, point_h, pair.at[1, own_pair]),
        fetch(2, skip_h, skip_full.at[own_skip]),
    ]
    first_inputs = [fetch(3, acts_h, acts), fetch(4, wk_h, wk), fetch(5, wv_h, wv), fetch(6, wq_h, wq)]
    later_inputs = [fetch(7, skips_h, skips), fetch(8, wo_h, wo)]

    ahead, behind = lax.rem(me + 1, places), lax.rem(me + places - 1, places)
    barrier = pltpu.get_barrier_semaphore()
    for place in (left, right, side, ahead, behind):
        pl.semaphore_signal(barrier, inc=1, device_id={"pos": place}, device_id_type=MESH)
    pl.semaphore_signal(barrier, inc=1, device_id={"group": partner}, device_id_type=MESH)
    pl.semaphore_wait(barrier, 6)

    for copy in shards:
        copy.wait()
    begin(MINE)
    begin(SKIP)
    begin(THEIRS)

    for copy in first_inputs:
        copy.wait()
    actsf = acts[...].astype(jnp.float32)
    centre = actsf - jnp.mean(actsf, axis=-1, keepdims=True)
    scale = lax.rsqrt(jnp.mean(centre * centre, axis=-1, keepdims=True) + 1e-05)
    normed[...] = (centre * scale * gain_ref[...]).astype(jnp.bfloat16)
    key_width = HEADS * HK

    def dot(a, b):
        return jnp.dot(a, b, preferred_element_type=jnp.float32)

    def dot_t(a, b):
        return lax.dot_general(a, b, (((1,), (1,)), ((), ())), preferred_element_type=jnp.float32)

    kv[me, :, 0:key_width] = dot(normed[...], wk[...]).astype(jnp.bfloat16)
    for tile in range(HEADS * HV // 256):
        kv[me, :, key_width + tile * 256 : key_width + tile * 256 + 256] = dot(
            normed[...], wv[:, tile * 256 : tile * 256 + 256]
        ).astype(jnp.bfloat16)
    begin(KV)
    queries[...] = (dot(normed[...], wq[...]) * HK ** (-0.5)).astype(jnp.bfloat16)

    for copy in later_inputs:
        copy.wait()
    pump(MINE, 1)
    pump(SKIP, 1)
    pump(KV, 1)

    @pl.loop(0, skips.shape[0] // 64)
    def _(step):
        rows = pl.ds(pl.multiple_of(step * 64, 64), 64)
        skip_act[rows] = jax.nn.gelu(skips[rows].astype(jnp.float32)).astype(jnp.bfloat16)

    for hops in range(2, reach + 1):
        pump(KV, hops)
        pump(MINE, hops)
        pump(SKIP, hops)
        if hops < reach:
            pump(THEIRS, hops - 1)
    from_side(KV)

    lane = lax.broadcasted_iota(jnp.int32, (bins, 2 * HK), 1)
    wide_lane = lax.broadcasted_iota(jnp.int32, (bins, 2 * HV), 1)
    keys_all = places * bins
    for seq in range(2):
        here = pl.ds(seq * bins, bins)
        for two in range(HEADS // 2):
            q = queries[here, two * 2 * HK : (two + 1) * 2 * HK]
            zero = jnp.zeros_like(q)
            both = jnp.concatenate([jnp.where(lane < HK, q, zero), jnp.where(lane < HK, zero, q)], axis=0)
            k = kv[:, here, two * 2 * HK : (two + 1) * 2 * HK].reshape(keys_all, 2 * HK)
            scores = dot_t(both, k)
            weights = jnp.exp(scores - jnp.max(scores, axis=-1, keepdims=True))
            totals = jnp.sum(weights, axis=-1, keepdims=True)
            value_at = key_width + two * 2 * HV
            v = kv[:, here, value_at : value_at + 2 * HV].reshape(keys_all, 2 * HV)
            summed = dot(weights.astype(jnp.bfloat16), v) / totals
            mixed[here, two * 2 * HV : (two + 1) * 2 * HV] = jnp.where(
                wide_lane < HV, summed[:bins], summed[bins:]
            ).astype(jnp.bfloat16)

    tiles = width // 256

    def tile_at(step):
        return pl.ds(pl.multiple_of(step * 256, 256), 256)

    @pl.loop(0, tiles)
    def _(step):
        cols = tile_at(step)
        attended = (acts[:, cols].astype(jnp.float32) + dot(mixed[...], wo[:, cols])).astype(jnp.bfloat16)
        activated[:, cols] = jax.nn.gelu(attended.astype(jnp.float32)).astype(jnp.bfloat16)

    for hops in range(max(reach - 1, 1), reach):
        pump(THEIRS, hops)
    from_side(SKIP)

    @pl.loop(0, tiles)
    def _(step):
        cols = tile_at(step)
        term[:, cols] = dot(skip_act[...], skip_full[:, cols])

    pump(THEIRS, reach)
    from_side(MINE)
    from_side(THEIRS)

    halo_out[...] = jnp.zeros_like(halo_out)
    ups = 2 * bins
    twice = (
        lax.div(lax.broadcasted_iota(jnp.int32, (2 * ups, 2 * bins), 0), 2)
        == lax.broadcasted_iota(jnp.int32, (2 * ups, 2 * bins), 1)
    ).astype(jnp.float32).astype(jnp.bfloat16)

    @pl.loop(0, tiles)
    def _(step):
        cols = tile_at(step)
        lifted = dot(activated[...], pair[0, :, cols]).astype(jnp.bfloat16)
        merged = (dot(twice, lifted) + term[:, cols]).astype(jnp.bfloat16).astype(jnp.float32)
        term[:, cols] = merged
        for seq in range(2):
            halo_out[0, seq : seq + 1, cols] = merged[seq * ups + ups - 1 : seq * ups + ups]
            halo_out[1, seq : seq + 1, cols] = merged[seq * ups : seq * ups + 1]

    edges = []
    for way, place in ((0, ahead), (1, behind)):
        copy = pltpu.make_async_remote_copy(
            src_ref=halo_out.at[way],
            dst_ref=halo_in.at[way],
            send_sem=halo_send.at[way],
            recv_sem=halo_recv.at[way],
            device_id={"pos": place},
            device_id_type=MESH,
        )
        copy.start()
        edges.append(copy)
    for copy in edges:
        copy.wait()

    row = lax.broadcasted_iota(jnp.int32, (ups, 256), 0)

    @pl.loop(0, tiles)
    def _(step):
        cols = tile_at(step)
        for seq in range(2):
            rows = pl.ds(seq * ups, ups)
            now = term[rows, cols]
            before = jnp.where(me > 0, halo_in[0, seq : seq + 1, cols], 0.0)
            after = jnp.where(me < places - 1, halo_in[1, seq : seq + 1, cols], 0.0)
            prev = jnp.where(row == 0, before, pltpu.roll(now, 1, 0))
            following = jnp.where(row == ups - 1, after, pltpu.roll(now, ups - 1, 0))
            spread[rows, cols] = (
                depth_ref[0:1, cols] * prev + depth_ref[1:2, cols] * now + depth_ref[2:3, cols] * following
            ).astype(jnp.bfloat16)

    @pl.loop(0, tiles)
    def _(step):
        cols = tile_at(step)
        out_ref[:, cols] = dot_t(spread[...], pair[1, cols, :]).astype(jnp.bfloat16)

    for copy in sent:
        copy.wait_send()


def fused(
    groups, places,
    acts, skips, norm_gain, w_query, w_key, w_value, w_out, w_lift, w_skip, depth_kernel, w_point
):
    seqs, bins, width = acts.shape
    ups, channels = skips.shape[1:]
    key_width, value_width = w_key.shape[1], w_value.shape[1]
    reach = places // 4
    slots = 2 * reach + 1
    bf, f32 = jnp.bfloat16, jnp.float32
    anywhere = pl.BlockSpec(memory_space=pl.ANY)
    vmem = pl.BlockSpec(memory_space=pltpu.VMEM)
    rows, up_rows = seqs * bins, seqs * ups
    out = pl.pallas_call(
        functools.partial(fused_kernel, groups, places),
        out_shape=jax.ShapeDtypeStruct((up_rows, width), bf),
        in_specs=[anywhere, anywhere, vmem] + [anywhere] * 7 + [vmem],
        out_specs=vmem,
        scratch_shapes=[
            pltpu.VMEM((rows, width), bf),
            pltpu.VMEM((up_rows, channels), bf),
            pltpu.VMEM((width, key_width), bf),
            pltpu.VMEM((width, key_width), bf),
            pltpu.VMEM((width, value_width), bf),
            pltpu.VMEM((value_width, width), bf),
            pltpu.VMEM((2, width, width), bf),
            pltpu.VMEM((channels, width), bf),
            pltpu.VMEM((places, rows, key_width + value_width), bf),
            pltpu.VMEM((rows, width), bf),
            pltpu.VMEM((rows, key_width), bf),
            pltpu.VMEM((rows, value_width), bf),
            pltpu.VMEM((rows, width), bf),
            pltpu.VMEM((up_rows, channels), bf),
            pltpu.VMEM((up_rows, width), f32),
            pltpu.VMEM((up_rows, width), bf),
            pltpu.VMEM((2, 8, width), f32),
            pltpu.VMEM((2, 8, width), f32),
            pltpu.SemaphoreType.DMA((9,)),
            pltpu.SemaphoreType.DMA((4, 3, slots)),
            pltpu.SemaphoreType.DMA((4, 2, slots)),
            pltpu.SemaphoreType.DMA((2,)),
            pltpu.SemaphoreType.DMA((2,)),
        ],
        compiler_params=pltpu.CompilerParams(
            collective_id=0, has_side_effects=True, vmem_limit_bytes=56 * 1024 * 1024
        ),
        cost_estimate=pl.CostEstimate(
            flops=4 * 10**9, bytes_accessed=3 * 10**7, transcendentals=10**6
        ),
    )(
        acts.reshape(rows, width),
        skips.reshape(up_rows, channels),
        norm_gain.reshape(1, width),
        w_query,
        w_key,
        w_value,
        w_out,
        w_lift,
        w_point.T,
        w_skip,
        depth_kernel,
    )
    return out.reshape(seqs, ups, width)


def suits(mesh, shapes):
    places, groups = mesh.shape["pos"], mesh.shape["group"]
    lift, skip = shapes
    return (
        places % 4 == 0
        and places <= 16
        and groups % 2 == 0
        and lift % places == 0
        and skip % places == 0
        and lift // places % 16 == 0
        and skip // places % 16 == 0
    )


def solution(mesh):
    specs = (
        P("group", "pos", None),
        P("group", "pos", None),
        P(),
        P(),
        P(),
        P(),
        P(),
        P("pos", None),
        P("pos", None),
        P(),
        P(None, "pos"),
    )

    def run(*args):
        body = on_device
        if suits(mesh, (args[7].shape[0], args[8].shape[0])):
            body = functools.partial(fused, mesh.shape["group"], mesh.shape["pos"])
        return jax.shard_map(
            body, mesh=mesh, in_specs=specs, out_specs=P("group", "pos", None), check_vma=False
        )(*args)

    return run
```

```python
import functools

import jax
import jax.numpy as jnp
from jax import lax
from jax.experimental import pallas as pl
from jax.experimental.pallas import tpu as pltpu
from jax.sharding import PartitionSpec as P

HEADS = 4
HK = 64
HV = 192


def extended(cells, sides, width):
    for axis, dim in sides:
        count = lax.axis_size(axis)
        ends = count - 1
        head = lax.slice_in_dim(cells, 0, width, axis=dim)
        tail = lax.slice_in_dim(cells, cells.shape[dim] - width, cells.shape[dim], axis=dim)
        cells = jnp.concatenate(
            [
                lax.ppermute(tail, axis, [(i, (i + 1) % count) for i in range(ends)]),
                cells,
                lax.ppermute(head, axis, [((i + 1) % count, i) for i in range(ends)]),
            ],
            axis=dim,
        )
    return cells


def on_device(
    acts, skips, norm_gain, w_query, w_key, w_value, w_out, w_lift, w_skip, depth_kernel, w_point
):
    lift_full, skip_full, point_full = (
        lax.all_gather(w_lift, "pos", axis=0, tiled=True),
        lax.all_gather(w_skip, "pos", axis=0, tiled=True),
        lax.all_gather(w_point, "pos", axis=1, tiled=True),
    )
    seq_count, bin_rows, width = acts.shape
    actsf = acts.astype(jnp.float32)
    centre = actsf - jnp.mean(actsf, axis=-1, keepdims=True)
    normed = (
        centre * lax.rsqrt(jnp.mean(centre * centre, axis=-1, keepdims=True) + 1e-05) * norm_gain
    ).astype(jnp.bfloat16)
    flat = normed.reshape(seq_count * bin_rows, width)
    queries = (
        (jnp.dot(flat, w_query, preferred_element_type=jnp.float32) * HK ** (-0.5))
        .astype(jnp.bfloat16)
        .reshape(seq_count, bin_rows, HEADS, HK)
    )
    keys_here = (
        jnp.dot(flat, w_key, preferred_element_type=jnp.float32)
        .astype(jnp.bfloat16)
        .reshape(seq_count, bin_rows, HEADS * HK)
    )
    values_here = (
        jnp.dot(flat, w_value, preferred_element_type=jnp.float32)
        .astype(jnp.bfloat16)
        .reshape(seq_count, bin_rows, HEADS * HV)
    )
    running = jnp.full((seq_count, HEADS, bin_rows), -1e30, jnp.float32)
    key_piece = lax.all_gather(keys_here, "pos", axis=1, tiled=True)
    value_piece = lax.all_gather(values_here, "pos", axis=1, tiled=True)
    count = key_piece.shape[1]
    keyed = key_piece.reshape(seq_count, count, HEADS, HK)
    valued = value_piece.reshape(seq_count, count, HEADS, HV)
    scores = jnp.einsum("sqhd,skhd->shqk", queries, keyed, preferred_element_type=jnp.float32)
    newest = jnp.maximum(running, jnp.max(scores, axis=-1))
    weights = jnp.exp(scores - newest[..., None])
    totals = jnp.sum(weights, axis=-1)
    summed = jnp.einsum(
        "shqk,skhv->shqv", weights.astype(jnp.bfloat16), valued, preferred_element_type=jnp.float32
    )
    running, totals, summed = (newest, totals, summed)
    mixed = (
        (summed / totals[..., None])
        .transpose(0, 2, 1, 3)
        .reshape(seq_count * bin_rows, HEADS * HV)
        .astype(jnp.bfloat16)
    )
    attended = (
        actsf.reshape(seq_count * bin_rows, width)
        + jnp.dot(mixed, w_out, preferred_element_type=jnp.float32)
    ).astype(jnp.bfloat16)
    activated = jax.nn.gelu(attended.astype(jnp.float32)).astype(jnp.bfloat16)
    lifted = jnp.dot(activated, lift_full, preferred_element_type=jnp.float32)
    lifted = lifted.astype(jnp.bfloat16).reshape(seq_count, bin_rows, width)
    raised = jnp.repeat(lifted, 2, axis=1).reshape(seq_count * 2 * bin_rows, width)
    skip_act = (
        jax.nn.gelu(skips.astype(jnp.float32))
        .astype(jnp.bfloat16)
        .reshape(seq_count * 2 * bin_rows, skips.shape[2])
    )
    skip_term = jnp.dot(skip_act, skip_full, preferred_element_type=jnp.float32)
    merged = (
        (raised.astype(jnp.float32) + skip_term)
        .astype(jnp.bfloat16)
        .reshape(seq_count, 2 * bin_rows, width)
    )
    padded = extended(merged, (("pos", 1),), 1)
    paddedf = padded.astype(jnp.float32)
    spread = (
        depth_kernel[0] * paddedf[:, :-2]
        + depth_kernel[1] * paddedf[:, 1:-1]
        + depth_kernel[2] * paddedf[:, 2:]
    ).astype(jnp.bfloat16)
    spread = spread.reshape(seq_count * 2 * bin_rows, width)
    decoded = jnp.dot(spread, point_full, preferred_element_type=jnp.float32)
    return decoded.astype(jnp.bfloat16).reshape(seq_count, 2 * bin_rows, width)


SEND_RING, SEND_SIDE, SEND_CROSS = 0, 1, 2
KV, SKIP, SKIP_MINE, SKIP_THEIRS, LIFT_MINE, LIFT_THEIRS, POINT_MINE, POINT_THEIRS = range(8)
MINE = (SKIP_MINE, LIFT_MINE, POINT_MINE)
THEIRS = (SKIP_THEIRS, LIFT_THEIRS, POINT_THEIRS)
ALONE = 16
MESH = pl.DeviceIdType.MESH


def fused_kernel(
    groups, places,
    acts_h, skips_h, gain_ref, wq_h, wk_h, wv_h, wo_h, lift_h, point_h, skip_h, depth_ref,
    out_ref,
    acts, skips, wq, wk, wv, wo, pair, skip_full, kv, normed, queries, mixed, activated,
    skip_act, term, spread, halo_out, halo_in,
    local_sem, send_sem, recv_sem, halo_send, halo_recv,
):
    chips = places // 2
    reach = chips // 2
    me, group = lax.axis_index("pos"), lax.axis_index("group")
    core, chip = lax.rem(me, 2), lax.div(me, 2)
    column, level = lax.rem(chip, 2), lax.div(chip, 2)
    ring = level + column * (chips - 1 - 2 * level)
    mine = lax.rem(group, 2)
    partner = group + 1 - 2 * mine
    side = chip * 2 + 1 - core
    width = acts.shape[1]
    skip_rows, pair_rows, bins = skip_h.shape[0], lift_h.shape[0], acts.shape[0] // 2

    def chip_at(place):
        place = lax.rem(place + chips, chips)
        far = lax.div(place, reach)
        return (1 - far) * 2 * place + far * (2 * (chips - 1 - place) + 1)

    right, left = chip_at(ring + 1) * 2 + core, chip_at(ring - 1) * 2 + core

    def origin(way, hops, of_core):
        return chip_at(ring - hops if way == 0 else ring + hops) * 2 + of_core

    def view(array, device, part):
        if array == KV:
            if part is None:
                return kv.at[device]
            return kv.at[device, pl.ds(part * bins, bins)]
        owned = mine if array in MINE else 1 - mine
        if array == SKIP:
            at, rows, first = 2 * ALONE, skip_rows - 2 * ALONE, (skip_rows // 2 - ALONE) // 16 * 16
        elif array in (SKIP_MINE, SKIP_THEIRS):
            at, rows, first = owned * ALONE, ALONE, ALONE
        else:
            half = pair_rows // 2
            low = half // 2 // 16 * 16
            at, rows = owned * half, half
            first = half - low if array in (LIFT_MINE, LIFT_THEIRS) else low
        start, size = ((0, rows), (0, first), (first, rows - first))[0 if part is None else part + 1]
        if array <= SKIP_THEIRS:
            return skip_full.at[pl.ds(pl.multiple_of(device * skip_rows + at + start, 16), size)]
        window = pl.ds(pl.multiple_of(device * pair_rows + at + start, 16), size)
        return pair.at[0 if array in (LIFT_MINE, LIFT_THEIRS) else 1, window]

    def absent(array, way, hops):
        return array in (SKIP_MINE, SKIP_THEIRS) and hops == reach and way == 1

    def slot(way, hops):
        return way * reach + hops - 1

    def part_of(way, hops):
        return way if hops == reach else None

    own_slot = 2 * reach
    sent = []

    def send(array, ref, kind, index, target, at_array=None):
        at_array = array if at_array is None else at_array
        copy = pltpu.make_async_remote_copy(
            src_ref=ref,
            dst_ref=ref,
            send_sem=send_sem.at[array, kind, index],
            recv_sem=recv_sem.at[at_array, 1 if kind == SEND_SIDE else 0, index],
            device_id=target,
            device_id_type=MESH,
        )
        copy.start()
        sent.append(copy)

    def arrived(array, plane, index, ref):
        pltpu.make_async_remote_copy(
            src_ref=ref,
            dst_ref=ref,
            send_sem=send_sem.at[array, 0, index],
            recv_sem=recv_sem.at[array, plane, index],
            device_id={"pos": side},
            device_id_type=MESH,
        ).wait_recv()

    def onward(array, way, hops):
        if hops < reach and not absent(array, way, hops + 1):
            ref = view(array, origin(way, hops, core), part_of(way, hops + 1))
            send(array, ref, SEND_RING, slot(way, hops + 1), {"pos": right if way == 0 else left})

    def pump(array, hops):
        for way in (0, 1):
            if absent(array, way, hops):
                continue
            ref = view(array, origin(way, hops, core), part_of(way, hops))
            arrived(array, 0, slot(way, hops), ref)
            if array not in THEIRS:
                onward(array, way, hops)
            if array in MINE:
                send(array, ref, SEND_CROSS, slot(way, hops), {"group": partner}, array + 1)
            send(array, ref, SEND_SIDE, slot(way, hops), {"pos": side})

    def begin(array):
        if array not in THEIRS:
            onward(array, 0, 0)
            onward(array, 1, 0)

    def begin_side(array):
        send(array, view(array, me, None), SEND_SIDE, own_slot, {"pos": side})

    def from_side(array):
        arrived(array, 1, own_slot, view(array, side, None))
        for hops in range(1, reach + 1):
            for way in (0, 1):
                if absent(array, way, hops):
                    continue
                ref = view(array, origin(way, hops, 1 - core), part_of(way, hops))
                arrived(array, 1, slot(way, hops), ref)

    def fetch(index, source, target):
        copy = pltpu.make_async_copy(source, target, local_sem.at[index])
        copy.start()
        return copy

    own_pair = pl.ds(pl.multiple_of(me * pair_rows, 16), pair_rows)
    own_skip = pl.ds(pl.multiple_of(me * skip_rows, 16), skip_rows)
    shards = [
        fetch(0, lift_h, pair.at[0, own_pair]),
        fetch(1, point_h, pair.at[1, own_pair]),
        fetch(2, skip_h, skip_full.at[own_skip]),
    ]
    first_inputs = [fetch(3, acts_h, acts), fetch(4, wk_h, wk), fetch(5, wv_h, wv), fetch(6, wq_h, wq)]
    later_inputs = [fetch(7, skips_h, skips), fetch(8, wo_h, wo)]

    ahead, behind = lax.rem(me + 1, places), lax.rem(me + places - 1, places)
    barrier = pltpu.get_barrier_semaphore()
    for place in (left, right, side, ahead, behind):
        pl.semaphore_signal(barrier, inc=1, device_id={"pos": place}, device_id_type=MESH)
    pl.semaphore_signal(barrier, inc=1, device_id={"group": partner}, device_id_type=MESH)
    pl.semaphore_wait(barrier, 6)

    for copy in shards:
        copy.wait()
    for array in (LIFT_MINE, SKIP_MINE, POINT_MINE, SKIP):
        begin(array)
    for array in range(SKIP, POINT_THEIRS + 1):
        begin_side(array)

    for copy in first_inputs:
        copy.wait()
    actsf = acts[...].astype(jnp.float32)
    centre = actsf - jnp.mean(actsf, axis=-1, keepdims=True)
    scale = lax.rsqrt(jnp.mean(centre * centre, axis=-1, keepdims=True) + 1e-05)
    normed[...] = (centre * scale * gain_ref[...].reshape(1, -1)).astype(jnp.bfloat16)
    key_width = HEADS * HK

    def dot(a, b):
        return jnp.dot(a, b, preferred_element_type=jnp.float32)

    def dot_t(a, b):
        return lax.dot_general(a, b, (((1,), (1,)), ((), ())), preferred_element_type=jnp.float32)

    kv[me, :, 0:key_width] = dot(normed[...], wk[...]).astype(jnp.bfloat16)
    for tile in range(HEADS * HV // 256):
        kv[me, :, key_width + tile * 256 : key_width + tile * 256 + 256] = dot(
            normed[...], wv[:, tile * 256 : tile * 256 + 256]
        ).astype(jnp.bfloat16)
    begin(KV)
    begin_side(KV)
    queries[...] = (dot(normed[...], wq[...]) * HK ** (-0.5)).astype(jnp.bfloat16)

    for copy in later_inputs:
        copy.wait()
    for array in (LIFT_MINE, SKIP_MINE, POINT_MINE, SKIP, KV):
        pump(array, 1)

    @pl.loop(0, skips.shape[0] // 64)
    def _(step):
        rows = pl.ds(pl.multiple_of(step * 64, 64), 64)
        skip_act[rows] = jax.nn.gelu(skips[rows].astype(jnp.float32)).astype(jnp.bfloat16)

    for hops in range(2, reach + 1):
        order = (LIFT_MINE, SKIP_MINE, KV, POINT_MINE, SKIP)
        for array in order if hops < reach else (KV, LIFT_MINE, SKIP_MINE, POINT_MINE, SKIP):
            pump(array, hops)
        if hops < reach:
            for array in THEIRS:
                pump(array, hops - 1)
    from_side(KV)

    lane = lax.broadcasted_iota(jnp.int32, (bins, 2 * HK), 1)
    wide_lane = lax.broadcasted_iota(jnp.int32, (bins, 2 * HV), 1)
    keys_all = places * bins
    for seq in range(2):
        here = pl.ds(seq * bins, bins)
        for two in range(HEADS // 2):
            q = queries[here, two * 2 * HK : (two + 1) * 2 * HK]
            zero = jnp.zeros_like(q)
            both = jnp.concatenate([jnp.where(lane < HK, q, zero), jnp.where(lane < HK, zero, q)], axis=0)
            k = kv[:, here, two * 2 * HK : (two + 1) * 2 * HK].reshape(keys_all, 2 * HK)
            scores = dot_t(both, k)
            weights = jnp.exp(scores - jnp.max(scores, axis=-1, keepdims=True))
            totals = jnp.sum(weights, axis=-1, keepdims=True)
            value_at = key_width + two * 2 * HV
            v = kv[:, here, value_at : value_at + 2 * HV].reshape(keys_all, 2 * HV)
            summed = dot(weights.astype(jnp.bfloat16), v) / totals
            mixed[here, two * 2 * HV : (two + 1) * 2 * HV] = jnp.where(
                wide_lane < HV, summed[:bins], summed[bins:]
            ).astype(jnp.bfloat16)

    tiles = width // 256

    def tile_at(step):
        return pl.ds(pl.multiple_of(step * 256, 256), 256)

    @pl.loop(0, tiles)
    def _(step):
        cols = tile_at(step)
        attended = (acts[:, cols].astype(jnp.float32) + dot(mixed[...], wo[:, cols])).astype(jnp.bfloat16)
        activated[:, cols] = jax.nn.gelu(attended.astype(jnp.float32)).astype(jnp.bfloat16)

    for hops in range(max(reach - 1, 1), reach):
        for array in THEIRS:
            pump(array, hops)
    pump(SKIP_THEIRS, reach)
    pump(LIFT_THEIRS, reach)
    for array in (SKIP, SKIP_MINE, SKIP_THEIRS):
        from_side(array)

    @pl.loop(0, tiles)
    def _(step):
        cols = tile_at(step)
        term[:, cols] = dot(skip_act[...], skip_full[:, cols])

    pump(POINT_THEIRS, reach)
    from_side(LIFT_MINE)
    from_side(LIFT_THEIRS)

    halo_out[...] = jnp.zeros_like(halo_out)
    ups = 2 * bins
    twice = (
        lax.div(lax.broadcasted_iota(jnp.int32, (2 * ups, 2 * bins), 0), 2)
        == lax.broadcasted_iota(jnp.int32, (2 * ups, 2 * bins), 1)
    ).astype(jnp.float32).astype(jnp.bfloat16)

    @pl.loop(0, tiles)
    def _(step):
        cols = tile_at(step)
        lifted = dot(activated[...], pair[0, :, cols]).astype(jnp.bfloat16)
        merged = (dot(twice, lifted) + term[:, cols]).astype(jnp.bfloat16).astype(jnp.float32)
        term[:, cols] = merged
        for seq in range(2):
            halo_out[0, seq : seq + 1, cols] = merged[seq * ups + ups - 1 : seq * ups + ups]
            halo_out[1, seq : seq + 1, cols] = merged[seq * ups : seq * ups + 1]

    edges = []
    for way, place in ((0, ahead), (1, behind)):
        copy = pltpu.make_async_remote_copy(
            src_ref=halo_out.at[way],
            dst_ref=halo_in.at[way],
            send_sem=halo_send.at[way],
            recv_sem=halo_recv.at[way],
            device_id={"pos": place},
            device_id_type=MESH,
        )
        copy.start()
        edges.append(copy)
    for copy in edges:
        copy.wait()

    row = lax.broadcasted_iota(jnp.int32, (ups, 256), 0)

    @pl.loop(0, tiles)
    def _(step):
        cols = tile_at(step)
        for seq in range(2):
            rows = pl.ds(seq * ups, ups)
            now = term[rows, cols]
            before = jnp.where(me > 0, halo_in[0, seq : seq + 1, cols], 0.0)
            after = jnp.where(me < places - 1, halo_in[1, seq : seq + 1, cols], 0.0)
            prev = jnp.where(row == 0, before, pltpu.roll(now, 1, 0))
            following = jnp.where(row == ups - 1, after, pltpu.roll(now, ups - 1, 0))
            spread[rows, cols] = (
                depth_ref[0:1, cols] * prev + depth_ref[1:2, cols] * now + depth_ref[2:3, cols] * following
            ).astype(jnp.bfloat16)

    from_side(POINT_MINE)
    from_side(POINT_THEIRS)

    @pl.loop(0, tiles)
    def _(step):
        cols = tile_at(step)
        out_ref[:, cols] = dot_t(spread[...], pair[1, cols, :]).astype(jnp.bfloat16)

    for copy in sent:
        copy.wait_send()


def fused(
    groups, places,
    acts, skips, norm_gain, w_query, w_key, w_value, w_out, w_lift, w_skip, depth_kernel, w_point
):
    seqs, bins, width = acts.shape
    ups, channels = skips.shape[1:]
    key_width, value_width = w_key.shape[1], w_value.shape[1]
    reach = places // 4
    slots = 2 * reach + 1
    bf, f32 = jnp.bfloat16, jnp.float32
    anywhere = pl.BlockSpec(memory_space=pl.ANY)
    vmem = pl.BlockSpec(memory_space=pltpu.VMEM)
    rows, up_rows = seqs * bins, seqs * ups
    out = pl.pallas_call(
        functools.partial(fused_kernel, groups, places),
        out_shape=jax.ShapeDtypeStruct((up_rows, width), bf),
        in_specs=[anywhere, anywhere, vmem] + [anywhere] * 7 + [vmem],
        out_specs=vmem,
        scratch_shapes=[
            pltpu.VMEM((rows, width), bf),
            pltpu.VMEM((up_rows, channels), bf),
            pltpu.VMEM((width, key_width), bf),
            pltpu.VMEM((width, key_width), bf),
            pltpu.VMEM((width, value_width), bf),
            pltpu.VMEM((value_width, width), bf),
            pltpu.VMEM((2, width, width), bf),
            pltpu.VMEM((channels, width), bf),
            pltpu.VMEM((places, rows, key_width + value_width), bf),
            pltpu.VMEM((rows, width), bf),
            pltpu.VMEM((rows, key_width), bf),
            pltpu.VMEM((rows, value_width), bf),
            pltpu.VMEM((rows, width), bf),
            pltpu.VMEM((up_rows, channels), bf),
            pltpu.VMEM((up_rows, width), f32),
            pltpu.VMEM((up_rows, width), bf),
            pltpu.VMEM((2, 8, width), f32),
            pltpu.VMEM((2, 8, width), f32),
            pltpu.SemaphoreType.DMA((9,)),
            pltpu.SemaphoreType.DMA((8, 3, slots)),
            pltpu.SemaphoreType.DMA((8, 2, slots)),
            pltpu.SemaphoreType.DMA((2,)),
            pltpu.SemaphoreType.DMA((2,)),
        ],
        compiler_params=pltpu.CompilerParams(
            collective_id=0, has_side_effects=True, vmem_limit_bytes=56 * 1024 * 1024
        ),
        cost_estimate=pl.CostEstimate(
            flops=4 * 10**9, bytes_accessed=3 * 10**7, transcendentals=10**6
        ),
    )(
        acts.reshape(rows, width),
        skips.reshape(up_rows, channels),
        norm_gain,
        w_query,
        w_key,
        w_value,
        w_out,
        w_lift,
        w_point.T,
        w_skip,
        depth_kernel,
    )
    return out.reshape(seqs, ups, width)


def suits(mesh, shapes):
    places, groups = mesh.shape["pos"], mesh.shape["group"]
    lift, skip = shapes
    return (
        places % 4 == 0
        and places <= 16
        and groups % 2 == 0
        and lift % places == 0
        and skip % places == 0
        and lift // places % 16 == 0
        and skip // places % 16 == 0
        and skip // places >= 64
        and lift // places % 32 == 0
        and lift // places >= 64
    )


def solution(mesh):
    specs = (
        P("group", "pos", None),
        P("group", "pos", None),
        P(),
        P(),
        P(),
        P(),
        P(),
        P("pos", None),
        P("pos", None),
        P(),
        P(None, "pos"),
    )

    def run(*args):
        body = on_device
        if suits(mesh, (args[7].shape[0], args[8].shape[0])):
            body = functools.partial(fused, mesh.shape["group"], mesh.shape["pos"])
        return jax.shard_map(
            body, mesh=mesh, in_specs=specs, out_specs=P("group", "pos", None), check_vma=False
        )(*args)

    return run
```
